512 devices in a mesh: chan: 128 (over z, y_hi, x), seg: 4 (over y_lo, core).
Axes of the slice: x: 4, y: 8 (y_hi: 4, y_lo: 2; y = y_hi * 2 + y_lo), z: 8, core: 2. Of those that a mesh axis runs over, the one named last changes fastest.
Arguments:
- strain: float32 [10240, 4096], P('chan', 'seg'), may hold values from -100 to 100, as said below
- alive_flags: int32 [10240, 4], P('chan', 'seg'), may hold values 0 or 1
- plan: int32 [128], replicated, may hold values from 0 to 127, each once
Outputs:
- stacked: bfloat16 [320, 327680], P('seg', 'chan')
The draws below stay inside these ranges and needn't reach their ends.
Inputs may be any that keep to these rules, and one draw needn't show every extreme that they name: `strain`: the traffic-noise record of each channel; amplitudes vary between channels and over time. `alive_flags`: 1 marks a live channel in a window. `plan`: each of the 128 channel blocks appears once; the first 4 entries name the source blocks in order.
All inputs are finite; a program needn't handle non-finite values. No bound on the sum of `alive_flags` on one device may be relied on, other than what follows from the above.
Results may differ from the reference program's by a relative error of at most 0.011.
Values may be sent and summed in bfloat16 or wider, within the bound.
No kernel may reach another device: no remote copies, remote signals or barrier semaphores. Data moves between devices by JAX's collectives and lax.ppermute only.
A program may use at most 64 MiB of HBM per device.

```python
import math
import jax
import jax.numpy as jnp
import numpy as np
from jax import lax

CH_DEV = 80
WIN = 1024
WIN_DEV = 1
LAGS = 32
STEPS = 4
SMOOTH = 64
BLOCKS = 128
CHANNELS = 10240
WINDOWS = 4
SAMPLES = 4096
SOURCES = 320
N_SEG = 4


def draw_strain(key, part):
    noise_key, envelope_key, wave_key = jax.random.split(key, 3)
    log_top = math.log(10.0)
    noise_part = jnp.clip(jax.random.normal(noise_key, (CHANNELS, SAMPLES), jnp.float32), -4.0, 4.0)
    weight = 0.8
    envelope = jnp.exp(jax.random.uniform(envelope_key, (CHANNELS, SAMPLES // 64), jnp.float32, 0.0, log_top))
    envelope = jnp.repeat(envelope, 64, axis=1)
    wavefield = jnp.clip(jax.random.normal(wave_key, (SAMPLES + LAGS,), jnp.float32), -4.0, 4.0)
    delays = jnp.arange(CHANNELS, dtype=jnp.int32) * 5 % (LAGS // 2)
    sample_index = jnp.arange(SAMPLES, dtype=jnp.int32)[None, :] + delays[:, None]
    coherent = wavefield[sample_index]
    return (envelope * (0.6 * noise_part + weight * coherent)).astype(jnp.float32)


def touch_ends(drawn, rng, smallest, largest):
    spot = [jax.random.randint(jax.random.fold_in(rng, axis), (), 0, length) for axis, length in enumerate(drawn.shape)]
    main_axis = drawn.shape.index(max(drawn.shape))
    neighbour = spot[:main_axis] + [(spot[main_axis] + 1) % drawn.shape[main_axis]] + spot[main_axis + 1:]
    return drawn.at[tuple(spot)].set(smallest).at[tuple(neighbour)].set(largest)


def setup_inputs(seed: int = 0) -> dict:
    streams_of = jax.random.split(jax.random.key(seed), 4)
    strain = draw_strain(jax.random.fold_in(streams_of[3], 71), 0)
    alive_flags = touch_ends((jax.random.randint(streams_of[1], (CHANNELS, WINDOWS), 0, 4) < 3).astype(jnp.int32), jax.random.fold_in(streams_of[1], 1), 0, 1)
    plan = jax.random.permutation(streams_of[2], BLOCKS).astype(jnp.int32)
    return {"strain": strain, "alive_flags": alive_flags, "plan": plan}


def reference(strain, alive_flags, plan):
    records = strain.reshape(CHANNELS, WINDOWS, WIN)
    magnitude = jnp.abs(records)
    running = jnp.concatenate([jnp.zeros((CHANNELS, WINDOWS, 1), jnp.float32), jnp.cumsum(magnitude, axis=2)], axis=2)
    position = np.arange(WIN)
    upper_end = np.minimum(position + SMOOTH, WIN - 1) + 1
    lower_end = np.maximum(position - SMOOTH, 0)
    level = (running[:, :, upper_end] - running[:, :, lower_end]) / jnp.asarray(upper_end - lower_end, jnp.float32)
    live_mask = alive_flags.astype(jnp.float32)
    normed = (records / (level + 1e-5) * live_mask[:, :, None]).astype(jnp.bfloat16)
    source_rows = (plan[:STEPS, None] * CH_DEV + jnp.arange(CH_DEV, dtype=jnp.int32)[None, :]).reshape(-1)
    sources = normed[source_rows]
    source_live = live_mask[source_rows]
    padded = jnp.pad(normed, ((0, 0), (0, 0), (LAGS // 2, LAGS // 2)))
    left_side = sources.astype(jnp.float32).reshape(SOURCES, N_SEG, WIN_DEV * WIN)

    def one_offset(offset):
        shifted = lax.dynamic_slice_in_dim(padded, offset, WIN, axis=2)
        right_side = shifted.astype(jnp.float32).reshape(CHANNELS, N_SEG, WIN_DEV * WIN)
        partial_value = jnp.einsum("sgt,rgt->gsr", left_side, right_side) / WIN
        partial_value = lax.optimization_barrier(partial_value.astype(jnp.bfloat16)).astype(jnp.float32)
        return jnp.sum(partial_value, axis=0)

    summed = lax.map(one_offset, jnp.arange(LAGS, dtype=jnp.int32))
    pairs_count = jnp.dot(source_live, live_mask.T, preferred_element_type=jnp.float32)
    stacked = jnp.transpose(summed, (1, 2, 0)) / jnp.maximum(pairs_count, 1.0)[:, :, None]
    return stacked.reshape(SOURCES, CHANNELS * LAGS).astype(jnp.bfloat16)
```

```python
import jax
import jax.numpy as jnp
from jax import lax
from jax.experimental import pallas as pl
from jax.experimental.pallas import tpu as pltpu
from jax.sharding import Mesh, PartitionSpec as P

CH = 80
WIN = 1024
WINDOWS = 4
LAGS = 32
SMOOTH = 64
FINE = 4
COARSE = LAGS // FINE
PAD = WIN + 128
PIECES = 32
ROWS = 20
PIECE_ROWS = 24
SENT_ROWS = 88
GROUP = 16
GROUPS = CH // GROUP

CHAN = ("z", "yh", "x")
SEG = ("yl", "core")
SCATTER = ("z", "x")
CROSS = ("yh", "yl", "core")

F32 = jnp.float32
BF16 = jnp.bfloat16
VMEM_LIMIT = 48 * 1024 * 1024


def iota(shape, dim):
    return lax.broadcasted_iota(jnp.int32, shape, dim)


def to_column(row, rows):
    width = row.shape[1]
    spread = jnp.broadcast_to(row, (rows, width))
    diagonal = iota((rows, width), 0) == iota((rows, width), 1)
    return jnp.sum(jnp.where(diagonal, spread, 0.0), axis=1, keepdims=True)


def norm_kernel(strain_ref, alive_ref, pieces_ref, own_ref, full, flags):
    live_row = alive_ref[...].astype(F32)
    live_col = to_column(live_row, CH)
    flags[...] = jnp.zeros((8, 128), F32)
    flags[0:1, 0:CH] = live_row
    position = iota((1, WIN), 1)
    samples_in = (
        jnp.minimum(position, SMOOTH) + jnp.minimum(WIN - 1 - position, SMOOTH) + 1
    ).astype(F32)
    for start in range(0, CH, 16):
        x = strain_ref[start : start + 16, :]
        magnitude = jnp.concatenate([jnp.abs(x), jnp.zeros((16, PAD - WIN), F32)], axis=1)
        total = magnitude
        width = 1
        while width < 2 * SMOOTH:
            total = total + pltpu.roll(total, PAD - width, 1)
            width *= 2
        total = pltpu.roll(total, SMOOTH, 1) + pltpu.roll(magnitude, PAD - SMOOTH, 1)
        level = total[:, :WIN] / samples_in
        normed = x / (level + 1e-5) * live_col[start : start + 16]
        full[start : start + 16, :] = normed
        own_ref[start : start + 16, :] = normed.astype(BF16)
    own_ref[CH : CH + 16, :] = jnp.zeros((16, WIN), BF16)
    own_ref[CH : CH + 16, 0:128] = jnp.concatenate(
        [flags[...], jnp.zeros((8, 128), F32)], axis=0
    ).astype(BF16)
    flag_rows = flags[0 : PIECE_ROWS - ROWS, :]
    for piece in range(PIECES):
        h, q = piece // 8, piece % 8
        data = full[h * ROWS : (h + 1) * ROWS, q * 128 : (q + 1) * 128]
        pieces_ref[piece] = jnp.concatenate([data, flag_rows], axis=0).astype(BF16)


def pick_kernel(plan_ref, got_ref, out_ref):
    for k in range(4):
        block = plan_ref[k]
        holder = (block // 16) * 4 + block % 4
        value = got_ref[holder]
        for y in range(4):
            out_ref[y * 4 + k] = value


def fan_kernel(plan_ref, seg_ref, got_ref, out_ref):
    block = plan_ref[seg_ref[0]]
    y = (block // 4) % 4
    pieces = [got_ref[y * 4 + w].astype(F32) for w in range(WINDOWS)]
    rows = [p[:ROWS] for p in pieces] + [p[ROWS : ROWS + 1] for p in pieces]
    rows.append(jnp.zeros((SENT_ROWS - WINDOWS * (ROWS + 1), 128), F32))
    value = jnp.concatenate(rows, axis=0).astype(BF16)
    for piece in range(PIECES):
        out_ref[piece] = value


def correlate_kernel(got_ref, own_ref, out_ref, source, lhs, rhs, total, order):
    row = iota((4 * 128, 4 * 128), 0)
    target = (row % 16) * LAGS + (row // 16 % 8) * FINE + row // 128
    order[...] = (iota((4 * 128, 4 * 128), 1) == target).astype(F32).astype(BF16)
    source[:, :, WIN:] = jnp.zeros((WINDOWS, CH, PAD - WIN), F32)
    for piece in range(PIECES):
        h, q = piece // 8, piece % 8
        value = got_ref[piece].astype(F32)
        for w in range(WINDOWS):
            source[w, h * ROWS : (h + 1) * ROWS, q * 128 : (q + 1) * 128] = value[
                w * ROWS : (w + 1) * ROWS
            ]
    for w in range(WINDOWS):
        block = source[w]
        for a in range(FINE):
            moved = block if a == 0 else pltpu.roll(block, a, 1)
            lhs[a * CH : (a + 1) * CH, :] = moved.astype(BF16)
        for g in range(GROUPS):
            own = own_ref[w, g * GROUP : (g + 1) * GROUP, :].astype(F32)
            own = jnp.concatenate([own, jnp.zeros((GROUP, PAD - WIN), F32)], axis=1)
            for b in range(COARSE):
                shift = (LAGS // 2 - FINE * b) % PAD
                moved = own if shift == 0 else pltpu.roll(own, shift, 1)
                first = g * 128 + b * GROUP
                rhs[first : first + GROUP, :] = moved.astype(BF16)
        partial = lax.dot_general(
            lhs[...], rhs[...], (((1,), (1,)), ((), ())), preferred_element_type=F32
        )
        partial = (partial * (1.0 / WIN)).astype(BF16).astype(F32)
        if w == 0:
            total[...] = partial
        else:
            total[...] += partial
    sent_flags = got_ref[0].astype(F32)[WINDOWS * ROWS : WINDOWS * (ROWS + 1)]
    lane = iota((128, GROUPS * 128), 1)
    channel = (lane // 128) * GROUP + lane % GROUP
    widen = (iota((128, GROUPS * 128), 0) == channel).astype(F32).astype(BF16)
    pairs = jnp.zeros((CH, GROUPS * 128), F32)
    for w in range(WINDOWS):
        own_flags = own_ref[w, CH : CH + 16, 0:128]
        wide = jnp.dot(own_flags, widen, preferred_element_type=F32)[0:1]
        pairs = pairs + to_column(sent_flags[w : w + 1], CH) * wide
    pairs = jnp.maximum(pairs, 1.0)
    scaled = [
        (total[a * CH : (a + 1) * CH, :] / pairs).astype(BF16) for a in range(FINE)
    ]
    for g in range(GROUPS):
        mixed = jnp.concatenate([s[:, g * 128 : (g + 1) * 128] for s in scaled], axis=1)
        out_ref[:, g * 512 : (g + 1) * 512] = jnp.dot(
            mixed, order[...], preferred_element_type=F32
        ).astype(BF16)


def vmem():
    return pl.BlockSpec(memory_space=pltpu.VMEM)


def smem():
    return pl.BlockSpec(memory_space=pltpu.SMEM)


def params():
    return pltpu.CompilerParams(vmem_limit_bytes=VMEM_LIMIT)


def per_device(strain, alive_flags, plan):
    pieces, own = pl.pallas_call(
        norm_kernel,
        out_shape=(
            jax.ShapeDtypeStruct((PIECES, PIECE_ROWS, 128), BF16),
            jax.ShapeDtypeStruct((CH + 16, WIN), BF16),
        ),
        in_specs=[vmem(), vmem()],
        out_specs=(vmem(), vmem()),
        scratch_shapes=[pltpu.VMEM((CH, WIN), F32), pltpu.VMEM((8, 128), F32)],
        compiler_params=params(),
    )(strain, alive_flags.reshape(1, CH))
    segment = (lax.axis_index("yl") * 2 + lax.axis_index("core")).astype(jnp.int32).reshape(1)
    scattered = lax.all_to_all(pieces, SCATTER, 0, 0, tiled=True)
    windows = lax.all_gather(own, SEG, axis=0)
    picked = pl.pallas_call(
        pick_kernel,
        out_shape=jax.ShapeDtypeStruct((16, PIECE_ROWS, 128), BF16),
        in_specs=[smem(), vmem()],
        out_specs=vmem(),
        compiler_params=params(),
    )(plan, scattered)
    crossed = lax.all_to_all(picked, CROSS, 0, 0, tiled=True)
    fanned = pl.pallas_call(
        fan_kernel,
        out_shape=jax.ShapeDtypeStruct((PIECES, SENT_ROWS, 128), BF16),
        in_specs=[smem(), smem(), vmem()],
        out_specs=vmem(),
        compiler_params=params(),
    )(plan, segment, crossed)
    gathered = lax.all_to_all(fanned, SCATTER, 0, 0, tiled=True)
    return pl.pallas_call(
        correlate_kernel,
        out_shape=jax.ShapeDtypeStruct((CH, CH * LAGS), BF16),
        in_specs=[vmem(), vmem()],
        out_specs=vmem(),
        scratch_shapes=[
            pltpu.VMEM((WINDOWS, CH, PAD), F32),
            pltpu.VMEM((FINE * CH, PAD), BF16),
            pltpu.VMEM((GROUPS * 128, PAD), BF16),
            pltpu.VMEM((FINE * CH, GROUPS * 128), F32),
            pltpu.VMEM((512, 512), BF16),
        ],
        compiler_params=params(),
    )(gathered, windows)


def solution(mesh):
    parts = Mesh(mesh.devices.reshape(8, 4, 4, 2, 2), ("z", "yh", "x", "yl", "core"))
    return jax.shard_map(
        per_device,
        mesh=parts,
        in_specs=(P(CHAN, SEG), P(CHAN, SEG), P()),
        out_specs=P(SEG, CHAN),
        check_vma=False,
    )
```

```python
import jax
import jax.numpy as jnp
from jax import lax
from jax.experimental import pallas as pl
from jax.experimental.pallas import tpu as pltpu
from jax.sharding import Mesh, PartitionSpec as P

CH = 80
WIN = 1024
WINDOWS = 4
LAGS = 32
SMOOTH = 64
FINE = 4
COARSE = LAGS // FINE
PAD = WIN + 128
PIECES = 32
ROWS = 20
PIECE_ROWS = 24
SENT_ROWS = WINDOWS * ROWS
GROUP = 16
GROUPS = CH // GROUP

CHAN = ("z", "yh", "x")
SEG = ("yl", "core")
SCATTER = ("z", "x")
CROSS = ("yh", "yl", "core")

F32 = jnp.float32
BF16 = jnp.bfloat16
VMEM_LIMIT = 24 * 1024 * 1024


def iota(shape, dim):
    return lax.broadcasted_iota(jnp.int32, shape, dim)


def to_column(row, rows):
    width = row.shape[1]
    spread = jnp.broadcast_to(row, (rows, width))
    diagonal = iota((rows, width), 0) == iota((rows, width), 1)
    return jnp.sum(jnp.where(diagonal, spread, 0.0), axis=1, keepdims=True)


def norm_kernel(strain_ref, alive_ref, pieces_ref, own_ref, full, flags):
    live_row = alive_ref[...].astype(F32)
    live_col = to_column(live_row, CH)
    flags[...] = jnp.zeros((8, 128), F32)
    flags[0:1, 0:CH] = live_row
    position = iota((1, WIN), 1)
    samples_in = (
        jnp.minimum(position, SMOOTH) + jnp.minimum(WIN - 1 - position, SMOOTH) + 1
    ).astype(F32)
    for start in range(0, CH, 16):
        x = strain_ref[start : start + 16, :]
        magnitude = jnp.concatenate([jnp.abs(x), jnp.zeros((16, PAD - WIN), F32)], axis=1)
        total = magnitude
        width = 1
        while width < 2 * SMOOTH:
            total = total + pltpu.roll(total, PAD - width, 1)
            width *= 2
        total = pltpu.roll(total, SMOOTH, 1) + pltpu.roll(magnitude, PAD - SMOOTH, 1)
        level = total[:, :WIN] / samples_in
        normed = x / (level + 1e-5) * live_col[start : start + 16]
        full[start : start + 16, :] = normed
        own_ref[start : start + 16, :] = normed.astype(BF16)
    own_ref[CH : CH + 16, :] = jnp.zeros((16, WIN), BF16)
    own_ref[CH : CH + 16, 0:128] = jnp.concatenate(
        [flags[...], jnp.zeros((8, 128), F32)], axis=0
    ).astype(BF16)
    flag_rows = flags[0 : PIECE_ROWS - ROWS, :]
    for piece in range(PIECES):
        q, h = piece // 4, piece % 4
        data = full[h * ROWS : (h + 1) * ROWS, q * 128 : (q + 1) * 128]
        pieces_ref[piece] = jnp.concatenate([data, flag_rows], axis=0).astype(BF16)


def pick_kernel(plan_ref, got_ref, out_ref):
    for k in range(4):
        block = plan_ref[k]
        holder = (block // 16) * 4 + block % 4
        value = got_ref[holder]
        for y in range(4):
            out_ref[y * 4 + k] = value


def fan_kernel(plan_ref, got_ref, out_ref, flags_ref):
    pair = lax.axis_index("yl") * 2
    block = plan_ref[pair + lax.axis_index("core")]
    y = (block // 4) % 4
    pieces = [got_ref[y * 4 + w].astype(F32) for w in range(WINDOWS)]
    value = jnp.concatenate([p[:ROWS] for p in pieces], axis=0).astype(BF16)
    flag_rows = [p[ROWS : ROWS + 1] for p in pieces] + [jnp.zeros((4, 128), F32)]
    flags_ref[...] = jnp.concatenate(flag_rows, axis=0)
    for copy in range(out_ref.shape[0]):
        out_ref[copy] = value


def correlate_kernel(got_ref, own_ref, flags_ref, out_ref, source, lhs, rhs, total, order):
    row = iota((4 * 128, 4 * 128), 0)
    target = (row % 16) * LAGS + (row // 16 % 8) * FINE + row // 128
    order[...] = (iota((4 * 128, 4 * 128), 1) == target).astype(F32).astype(BF16)
    source[:, :, WIN:] = jnp.zeros((WINDOWS, CH, PAD - WIN), F32)
    for piece in range(PIECES):
        q, h = piece // 4, piece % 4
        value = got_ref[piece].astype(F32)
        for w in range(WINDOWS):
            source[w, h * ROWS : (h + 1) * ROWS, q * 128 : (q + 1) * 128] = value[
                w * ROWS : (w + 1) * ROWS
            ]
    for w in range(WINDOWS):
        block = source[w]
        for a in range(FINE):
            moved = block if a == 0 else pltpu.roll(block, a, 1)
            lhs[a * CH : (a + 1) * CH, :] = moved.astype(BF16)
        for g in range(GROUPS):
            own = own_ref[w, g * GROUP : (g + 1) * GROUP, :].astype(F32)
            own = jnp.concatenate([own, jnp.zeros((GROUP, PAD - WIN), F32)], axis=1)
            for b in range(COARSE):
                shift = (LAGS // 2 - FINE * b) % PAD
                moved = own if shift == 0 else pltpu.roll(own, shift, 1)
                first = g * 128 + b * GROUP
                rhs[first : first + GROUP, :] = moved.astype(BF16)
        partial = lax.dot_general(
            lhs[...], rhs[...], (((1,), (1,)), ((), ())), preferred_element_type=F32
        )
        partial = (partial * (1.0 / WIN)).astype(BF16).astype(F32)
        if w == 0:
            total[...] = partial
        else:
            total[...] += partial
    lane = iota((128, GROUPS * 128), 1)
    channel = (lane // 128) * GROUP + lane % GROUP
    widen = (iota((128, GROUPS * 128), 0) == channel).astype(F32).astype(BF16)
    pairs = jnp.zeros((CH, GROUPS * 128), F32)
    for w in range(WINDOWS):
        own_flags = own_ref[w, CH : CH + 16, 0:128]
        wide = jnp.dot(own_flags, widen, preferred_element_type=F32)[0:1]
        pairs = pairs + to_column(flags_ref[w : w + 1, :], CH) * wide
    pairs = jnp.maximum(pairs, 1.0)
    scaled = [
        (total[a * CH : (a + 1) * CH, :] / pairs).astype(BF16) for a in range(FINE)
    ]
    for g in range(GROUPS):
        mixed = jnp.concatenate([s[:, g * 128 : (g + 1) * 128] for s in scaled], axis=1)
        out_ref[:, g * 512 : (g + 1) * 512] = jnp.dot(
            mixed, order[...], preferred_element_type=F32
        ).astype(BF16)


def vmem():
    return pl.BlockSpec(memory_space=pltpu.VMEM)


def smem():
    return pl.BlockSpec(memory_space=pltpu.SMEM)


def params():
    return pltpu.CompilerParams(vmem_limit_bytes=VMEM_LIMIT)


def per_device(strain, alive_flags, plan):
    pieces, own = pl.pallas_call(
        norm_kernel,
        out_shape=(
            jax.ShapeDtypeStruct((PIECES, PIECE_ROWS, 128), BF16),
            jax.ShapeDtypeStruct((CH + 16, WIN), BF16),
        ),
        in_specs=[vmem(), vmem()],
        out_specs=(vmem(), vmem()),
        scratch_shapes=[pltpu.VMEM((CH, WIN), F32), pltpu.VMEM((8, 128), F32)],
        compiler_params=params(),
    )(strain, alive_flags.reshape(1, CH))
    scattered = lax.all_to_all(pieces, SCATTER, 0, 0, tiled=True)
    windows = lax.all_gather(own, SEG, axis=0)
    picked = pl.pallas_call(
        pick_kernel,
        out_shape=jax.ShapeDtypeStruct((16, PIECE_ROWS, 128), BF16),
        in_specs=[smem(), vmem()],
        out_specs=vmem(),
        compiler_params=params(),
    )(plan, scattered)
    crossed = lax.all_to_all(picked, CROSS, 0, 0, tiled=True)
    fanned, source_flags = pl.pallas_call(
        fan_kernel,
        out_shape=(
            jax.ShapeDtypeStruct((PIECES, SENT_ROWS, 128), BF16),
            jax.ShapeDtypeStruct((8, 128), F32),
        ),
        in_specs=[smem(), vmem()],
        out_specs=(vmem(), vmem()),
        compiler_params=params(),
    )(plan, crossed)
    gathered = lax.all_to_all(fanned, SCATTER, 0, 0, tiled=True)
    return pl.pallas_call(
        correlate_kernel,
        out_shape=jax.ShapeDtypeStruct((CH, CH * LAGS), BF16),
        in_specs=[vmem()] * 3,
        out_specs=vmem(),
        scratch_shapes=[
            pltpu.VMEM((WINDOWS, CH, PAD), F32),
            pltpu.VMEM((FINE * CH, PAD), BF16),
            pltpu.VMEM((GROUPS * 128, PAD), BF16),
            pltpu.VMEM((FINE * CH, GROUPS * 128), F32),
            pltpu.VMEM((512, 512), BF16),
        ],
        compiler_params=params(),
    )(gathered, windows, source_flags)


def solution(mesh):
    parts = Mesh(mesh.devices.reshape(8, 4, 4, 2, 2), ("z", "yh", "x", "yl", "core"))
    return jax.shard_map(
        per_device,
        mesh=parts,
        in_specs=(P(CHAN, SEG), P(CHAN, SEG), P()),
        out_specs=P(SEG, CHAN),
        check_vma=False,
    )
```

```python
import jax
import jax.numpy as jnp
from jax import lax
from jax.experimental import pallas as pl
from jax.experimental.pallas import tpu as pltpu
from jax.sharding import Mesh, PartitionSpec as P

CH = 80
WIN = 1024
WINDOWS = 4
LAGS = 32
SMOOTH = 64
FINE = 4
COARSE = LAGS // FINE
PAD = WIN + 128
PIECES = 32
ROWS = 20
PIECE_ROWS = 24
SENT_ROWS = WINDOWS * ROWS
GROUP = 16
GROUPS = CH // GROUP

CHAN = ("z", "yh", "x")
SEG = ("yl", "core")
SCATTER = ("z", "x")
CROSS = ("yh", "yl", "core")

F32 = jnp.float32
BF16 = jnp.bfloat16
VMEM_LIMIT = 24 * 1024 * 1024


def iota(shape, dim):
    return lax.broadcasted_iota(jnp.int32, shape, dim)


def to_column(row, rows):
    width = row.shape[1]
    spread = jnp.broadcast_to(row, (rows, width))
    diagonal = iota((rows, width), 0) == iota((rows, width), 1)
    return jnp.sum(jnp.where(diagonal, spread, 0.0), axis=1, keepdims=True)


def norm_kernel(strain_ref, alive_ref, pieces_ref, own_ref, full, flags):
    live_row = alive_ref[...].astype(F32)
    live_col = to_column(live_row, CH)
    flags[...] = jnp.zeros((8, 128), F32)
    flags[0:1, 0:CH] = live_row
    position = iota((1, WIN), 1)
    samples_in = (
        jnp.minimum(position, SMOOTH) + jnp.minimum(WIN - 1 - position, SMOOTH) + 1
    ).astype(F32)
    distance = iota((384, 128), 0) - iota((384, 128), 1) - 128
    band = (jnp.abs(distance) <= SMOOTH).astype(F32).astype(BF16)
    edge = jnp.zeros((16, 128), BF16)
    for start in range(0, CH, 16):
        x = strain_ref[start : start + 16, :]
        rest = jnp.abs(x)
        terms = []
        for _ in range(3):
            term = rest.astype(BF16)
            rest = rest - term.astype(F32)
            terms.append(jnp.concatenate([edge, term, edge], axis=1))
        spans = jnp.concatenate(
            [t[:, b * 128 : b * 128 + 384] for t in terms for b in range(8)], axis=0
        )
        sums = jnp.dot(spans, band, preferred_element_type=F32)
        sums = sums[0:128] + sums[128:256] + sums[256:384]
        total = jnp.concatenate([sums[b * 16 : (b + 1) * 16] for b in range(8)], axis=1)
        level = total / samples_in
        normed = x / (level + 1e-5) * live_col[start : start + 16]
        full[start : start + 16, :] = normed
        own_ref[start : start + 16, :] = normed.astype(BF16)
    own_ref[CH : CH + 16, :] = jnp.zeros((16, WIN), BF16)
    own_ref[CH : CH + 16, 0:128] = jnp.concatenate(
        [flags[...], jnp.zeros((8, 128), F32)], axis=0
    ).astype(BF16)
    flag_rows = flags[0 : PIECE_ROWS - ROWS, :]
    for piece in range(PIECES):
        q, h = piece // 4, piece % 4
        data = full[h * ROWS : (h + 1) * ROWS, q * 128 : (q + 1) * 128]
        pieces_ref[piece] = jnp.concatenate([data, flag_rows], axis=0).astype(BF16)


def pick_kernel(plan_ref, got_ref, out_ref):
    for k in range(4):
        block = plan_ref[k]
        holder = (block // 16) * 4 + block % 4
        value = got_ref[holder]
        for y in range(4):
            out_ref[y * 4 + k] = value


def fan_kernel(plan_ref, got_ref, out_ref, flags_ref):
    pair = lax.axis_index("yl") * 2
    block = plan_ref[pair + lax.axis_index("core")]
    y = (block // 4) % 4
    pieces = [got_ref[y * 4 + w].astype(F32) for w in range(WINDOWS)]
    value = jnp.concatenate([p[:ROWS] for p in pieces], axis=0).astype(BF16)
    flag_rows = [p[ROWS : ROWS + 1] for p in pieces] + [jnp.zeros((4, 128), F32)]
    flags_ref[...] = jnp.concatenate(flag_rows, axis=0)
    for copy in range(out_ref.shape[0]):
        out_ref[copy] = value


def correlate_kernel(
    got_ref, own_ref, flags_ref, out_hbm, source, lhs, rhs, total, order, out_ref, sems
):
    row = iota((4 * 128, 4 * 128), 0)
    target = (row % 16) * LAGS + (row // 16 % 8) * FINE + row // 128
    order[...] = (iota((4 * 128, 4 * 128), 1) == target).astype(F32).astype(BF16)
    for w in range(WINDOWS):
        for g in range(GROUPS):
            own = own_ref[w, g * GROUP : (g + 1) * GROUP, :].astype(F32)
            own = jnp.concatenate([own, jnp.zeros((GROUP, PAD - WIN), F32)], axis=1)
            for b in range(COARSE):
                shift = (LAGS // 2 - FINE * b) % PAD
                moved = own if shift == 0 else pltpu.roll(own, shift, 1)
                first = g * 128 + b * GROUP
                rhs[w, first : first + GROUP, :] = moved.astype(BF16)
    lane = iota((128, GROUPS * 128), 1)
    channel = (lane // 128) * GROUP + lane % GROUP
    widen = (iota((128, GROUPS * 128), 0) == channel).astype(F32).astype(BF16)
    pairs = jnp.zeros((CH, GROUPS * 128), F32)
    for w in range(WINDOWS):
        own_flags = own_ref[w, CH : CH + 16, 0:128]
        wide = jnp.dot(own_flags, widen, preferred_element_type=F32)[0:1]
        pairs = pairs + to_column(flags_ref[w : w + 1, :], CH) * wide
    pairs = jnp.maximum(pairs, 1.0)
    source[:, :, WIN:] = jnp.zeros((WINDOWS, CH, PAD - WIN), F32)
    for piece in range(PIECES):
        q, h = piece // 4, piece % 4
        value = got_ref[piece].astype(F32)
        for w in range(WINDOWS):
            source[w, h * ROWS : (h + 1) * ROWS, q * 128 : (q + 1) * 128] = value[
                w * ROWS : (w + 1) * ROWS
            ]
    for w in range(WINDOWS):
        block = source[w]
        for a in range(FINE):
            moved = block if a == 0 else pltpu.roll(block, a, 1)
            lhs[w, a * CH : (a + 1) * CH, :] = moved.astype(BF16)
    for w in range(WINDOWS):
        partial = lax.dot_general(
            lhs[w], rhs[w], (((1,), (1,)), ((), ())), preferred_element_type=F32
        )
        partial = (partial * (1.0 / WIN)).astype(BF16).astype(F32)
        if w == 0:
            total[...] = partial
        else:
            total[...] += partial
    scaled = [
        (total[a * CH : (a + 1) * CH, :] / pairs).astype(BF16) for a in range(FINE)
    ]
    copies = []
    for g in range(GROUPS):
        mixed = jnp.concatenate([s[:, g * 128 : (g + 1) * 128] for s in scaled], axis=1)
        columns = pl.ds(g * 512, 512)
        out_ref[:, columns] = jnp.dot(
            mixed, order[...], preferred_element_type=F32
        ).astype(BF16)
        copy = pltpu.make_async_copy(
            out_ref.at[:, columns], out_hbm.at[:, columns], sems.at[g]
        )
        copy.start()
        copies.append(copy)
    for copy in copies:
        copy.wait()


def vmem():
    return pl.BlockSpec(memory_space=pltpu.VMEM)


def smem():
    return pl.BlockSpec(memory_space=pltpu.SMEM)


def params():
    return pltpu.CompilerParams(vmem_limit_bytes=VMEM_LIMIT)


def per_device(strain, alive_flags, plan):
    pieces, own = pl.pallas_call(
        norm_kernel,
        out_shape=(
            jax.ShapeDtypeStruct((PIECES, PIECE_ROWS, 128), BF16),
            jax.ShapeDtypeStruct((CH + 16, WIN), BF16),
        ),
        in_specs=[vmem(), vmem()],
        out_specs=(vmem(), vmem()),
        scratch_shapes=[pltpu.VMEM((CH, WIN), F32), pltpu.VMEM((8, 128), F32)],
        compiler_params=params(),
    )(strain, alive_flags.reshape(1, CH))
    scattered = lax.all_to_all(pieces, SCATTER, 0, 0, tiled=True)
    windows = lax.all_gather(own, SEG, axis=0)
    picked = pl.pallas_call(
        pick_kernel,
        out_shape=jax.ShapeDtypeStruct((16, PIECE_ROWS, 128), BF16),
        in_specs=[smem(), vmem()],
        out_specs=vmem(),
        compiler_params=params(),
    )(plan, scattered)
    crossed = lax.all_to_all(picked, CROSS, 0, 0, tiled=True)
    fanned, source_flags = pl.pallas_call(
        fan_kernel,
        out_shape=(
            jax.ShapeDtypeStruct((PIECES, SENT_ROWS, 128), BF16),
            jax.ShapeDtypeStruct((8, 128), F32),
        ),
        in_specs=[smem(), vmem()],
        out_specs=(vmem(), vmem()),
        compiler_params=params(),
    )(plan, crossed)
    gathered = lax.all_to_all(fanned, SCATTER, 0, 0, tiled=True)
    return pl.pallas_call(
        correlate_kernel,
        out_shape=jax.ShapeDtypeStruct((CH, CH * LAGS), BF16),
        in_specs=[vmem()] * 3,
        out_specs=pl.BlockSpec(memory_space=pl.ANY),
        scratch_shapes=[
            pltpu.VMEM((WINDOWS, CH, PAD), F32),
            pltpu.VMEM((WINDOWS, FINE * CH, PAD), BF16),
            pltpu.VMEM((WINDOWS, GROUPS * 128, PAD), BF16),
            pltpu.VMEM((FINE * CH, GROUPS * 128), F32),
            pltpu.VMEM((512, 512), BF16),
            pltpu.VMEM((CH, CH * LAGS), BF16),
            pltpu.SemaphoreType.DMA((GROUPS,)),
        ],
        compiler_params=params(),
        cost_estimate=pl.CostEstimate(flops=3400000000, bytes_accessed=2000000, transcendentals=0),
    )(gathered, windows, source_flags)


def solution(mesh):
    parts = Mesh(mesh.devices.reshape(8, 4, 4, 2, 2), ("z", "yh", "x", "yl", "core"))
    return jax.shard_map(
        per_device,
        mesh=parts,
        in_specs=(P(CHAN, SEG), P(CHAN, SEG), P()),
        out_specs=P(SEG, CHAN),
        check_vma=False,
    )
```

```python
import jax
import jax.numpy as jnp
from jax import lax
from jax.experimental import pallas as pl
from jax.experimental.pallas import tpu as pltpu
from jax.sharding import Mesh, PartitionSpec as P

CH = 80
WIN = 1024
WINDOWS = 4
LAGS = 32
SMOOTH = 64
FINE = 4
COARSE = LAGS // FINE
PAD = WIN + 128
PIECES = 32
ROWS = 20
PIECE_ROWS = 24
SENT_ROWS = WINDOWS * ROWS
GROUP = 16
GROUPS = CH // GROUP

CHAN = ("z", "yh", "x")
SEG = ("yl", "core")
SCATTER = ("x", "z")
CROSS = ("yh", "yl", "core")

F32 = jnp.float32
BF16 = jnp.bfloat16
VMEM_LIMIT = 24 * 1024 * 1024


def iota(shape, dim):
    return lax.broadcasted_iota(jnp.int32, shape, dim)


def to_column(row, rows):
    width = row.shape[1]
    spread = jnp.broadcast_to(row, (rows, width))
    diagonal = iota((rows, width), 0) == iota((rows, width), 1)
    return jnp.sum(jnp.where(diagonal, spread, 0.0), axis=1, keepdims=True)


def norm_kernel(strain_ref, alive_ref, pieces_ref, own_ref, full, flags):
    live_row = alive_ref[...].astype(F32)
    live_col = to_column(live_row, CH)
    flags[...] = jnp.zeros((8, 128), F32)
    flags[0:1, 0:CH] = live_row
    position = iota((1, WIN), 1)
    samples_in = (
        jnp.minimum(position, SMOOTH) + jnp.minimum(WIN - 1 - position, SMOOTH) + 1
    ).astype(F32)
    distance = iota((384, 128), 0) - iota((384, 128), 1) - 128
    band = (jnp.abs(distance) <= SMOOTH).astype(F32).astype(BF16)
    edge = jnp.zeros((16, 128), BF16)
    for start in range(0, CH, 16):
        x = strain_ref[start : start + 16, :]
        rest = jnp.abs(x)
        terms = []
        for _ in range(3):
            term = rest.astype(BF16)
            rest = rest - term.astype(F32)
            terms.append(jnp.concatenate([edge, term, edge], axis=1))
        spans = jnp.concatenate(
            [t[:, b * 128 : b * 128 + 384] for t in terms for b in range(8)], axis=0
        )
        sums = jnp.dot(spans, band, preferred_element_type=F32)
        sums = sums[0:128] + sums[128:256] + sums[256:384]
        total = jnp.concatenate([sums[b * 16 : (b + 1) * 16] for b in range(8)], axis=1)
        level = total / samples_in
        normed = x / (level + 1e-5) * live_col[start : start + 16]
        full[start : start + 16, :] = normed
        own_ref[start : start + 16, :] = normed.astype(BF16)
    own_ref[CH : CH + 16, :] = jnp.zeros((16, WIN), BF16)
    own_ref[CH : CH + 16, 0:128] = jnp.concatenate(
        [flags[...], jnp.zeros((8, 128), F32)], axis=0
    ).astype(BF16)
    flag_rows = flags[0 : PIECE_ROWS - ROWS, :]
    for piece in range(PIECES):
        h, q = piece // 8, piece % 8
        data = full[h * ROWS : (h + 1) * ROWS, q * 128 : (q + 1) * 128]
        pieces_ref[piece] = jnp.concatenate([data, flag_rows], axis=0).astype(BF16)


def pick_kernel(plan_ref, got_ref, out_ref):
    for k in range(4):
        block = plan_ref[k]
        holder = (block % 4) * 8 + block // 16
        value = got_ref[holder]
        for y in range(4):
            out_ref[y * 4 + k] = value


def fan_kernel(plan_ref, got_ref, out_ref, flags_ref):
    pair = lax.axis_index("yl") * 2
    block = plan_ref[pair + lax.axis_index("core")]
    y = (block // 4) % 4
    pieces = [got_ref[y * 4 + w].astype(F32) for w in range(WINDOWS)]
    value = jnp.concatenate([p[:ROWS] for p in pieces], axis=0).astype(BF16)
    flag_rows = [p[ROWS : ROWS + 1] for p in pieces] + [jnp.zeros((4, 128), F32)]
    flags_ref[...] = jnp.concatenate(flag_rows, axis=0)
    for copy in range(out_ref.shape[0]):
        out_ref[copy] = value


def correlate_kernel(
    got_ref, own_ref, flags_ref, out_hbm, source, lhs, rhs, total, order, out_ref, sems
):
    row = iota((4 * 128, 4 * 128), 0)
    target = (row % 16) * LAGS + (row // 16 % 8) * FINE + row // 128
    order[...] = (iota((4 * 128, 4 * 128), 1) == target).astype(F32).astype(BF16)
    for w in range(WINDOWS):
        for g in range(GROUPS):
            own = own_ref[w, g * GROUP : (g + 1) * GROUP, :]
            own = jnp.concatenate([own, jnp.zeros((GROUP, PAD - WIN), BF16)], axis=1)
            for b in range(COARSE):
                shift = (LAGS // 2 - FINE * b) % PAD
                moved = own if shift == 0 else pltpu.roll(own, shift, 1)
                first = g * 128 + b * GROUP
                rhs[w, first : first + GROUP, :] = moved
    lane = iota((128, GROUPS * 128), 1)
    channel = (lane // 128) * GROUP + lane % GROUP
    widen = (iota((128, GROUPS * 128), 0) == channel).astype(F32).astype(BF16)
    pairs = jnp.zeros((CH, GROUPS * 128), F32)
    for w in range(WINDOWS):
        own_flags = own_ref[w, CH : CH + 16, 0:128]
        wide = jnp.dot(own_flags, widen, preferred_element_type=F32)[0:1]
        pairs = pairs + to_column(flags_ref[w : w + 1, :], CH) * wide
    pairs = jnp.maximum(pairs, 1.0)
    source[:, :, WIN:] = jnp.zeros((WINDOWS, CH, PAD - WIN), F32)
    for piece in range(PIECES):
        h, q = piece // 8, piece % 8
        value = got_ref[piece].astype(F32)
        for w in range(WINDOWS):
            source[w, h * ROWS : (h + 1) * ROWS, q * 128 : (q + 1) * 128] = value[
                w * ROWS : (w + 1) * ROWS
            ]
    for w in range(WINDOWS):
        block = source[w].astype(BF16)
        for a in range(FINE):
            moved = block if a == 0 else pltpu.roll(block, a, 1)
            lhs[w, a * CH : (a + 1) * CH, :] = moved
    for w in range(WINDOWS):
        partial = lax.dot_general(
            lhs[w], rhs[w], (((1,), (1,)), ((), ())), preferred_element_type=F32
        )
        partial = (partial * (1.0 / WIN)).astype(BF16).astype(F32)
        if w == 0:
            total[...] = partial
        else:
            total[...] += partial
    scaled = [
        (total[a * CH : (a + 1) * CH, :] / pairs).astype(BF16) for a in range(FINE)
    ]
    copies = []
    for g in range(GROUPS):
        mixed = jnp.concatenate([s[:, g * 128 : (g + 1) * 128] for s in scaled], axis=1)
        columns = pl.ds(g * 512, 512)
        out_ref[:, columns] = jnp.dot(
            mixed, order[...], preferred_element_type=F32
        ).astype(BF16)
        copy = pltpu.make_async_copy(
            out_ref.at[:, columns], out_hbm.at[:, columns], sems.at[g]
        )
        copy.start()
        copies.append(copy)
    for copy in copies:
        copy.wait()


def vmem():
    return pl.BlockSpec(memory_space=pltpu.VMEM)


def smem():
    return pl.BlockSpec(memory_space=pltpu.SMEM)


def params():
    return pltpu.CompilerParams(vmem_limit_bytes=VMEM_LIMIT)


def per_device(strain, alive_flags, plan):
    pieces, own = pl.pallas_call(
        norm_kernel,
        out_shape=(
            jax.ShapeDtypeStruct((PIECES, PIECE_ROWS, 128), BF16),
            jax.ShapeDtypeStruct((CH + 16, WIN), BF16),
        ),
        in_specs=[vmem(), vmem()],
        out_specs=(vmem(), vmem()),
        scratch_shapes=[pltpu.VMEM((CH, WIN), F32), pltpu.VMEM((8, 128), F32)],
        compiler_params=params(),
    )(strain, alive_flags.reshape(1, CH))
    scattered = lax.all_to_all(pieces, SCATTER, 0, 0, tiled=True)
    windows = lax.all_gather(own, SEG, axis=0)
    picked = pl.pallas_call(
        pick_kernel,
        out_shape=jax.ShapeDtypeStruct((16, PIECE_ROWS, 128), BF16),
        in_specs=[smem(), vmem()],
        out_specs=vmem(),
        compiler_params=params(),
    )(plan, scattered)
    crossed = lax.all_to_all(picked, CROSS, 0, 0, tiled=True)
    fanned, source_flags = pl.pallas_call(
        fan_kernel,
        out_shape=(
            jax.ShapeDtypeStruct((PIECES, SENT_ROWS, 128), BF16),
            jax.ShapeDtypeStruct((8, 128), F32),
        ),
        in_specs=[smem(), vmem()],
        out_specs=(vmem(), vmem()),
        compiler_params=params(),
    )(plan, crossed)
    gathered = lax.all_to_all(fanned, SCATTER, 0, 0, tiled=True)
    return pl.pallas_call(
        correlate_kernel,
        out_shape=jax.ShapeDtypeStruct((CH, CH * LAGS), BF16),
        in_specs=[vmem()] * 3,
        out_specs=pl.BlockSpec(memory_space=pl.ANY),
        scratch_shapes=[
            pltpu.VMEM((WINDOWS, CH, PAD), F32),
            pltpu.VMEM((WINDOWS, FINE * CH, PAD), BF16),
            pltpu.VMEM((WINDOWS, GROUPS * 128, PAD), BF16),
            pltpu.VMEM((FINE * CH, GROUPS * 128), F32),
            pltpu.VMEM((512, 512), BF16),
            pltpu.VMEM((CH, CH * LAGS), BF16),
            pltpu.SemaphoreType.DMA((GROUPS,)),
        ],
        compiler_params=params(),
        cost_estimate=pl.CostEstimate(flops=3400000000, bytes_accessed=2000000, transcendentals=0),
    )(gathered, windows, source_flags)


def solution(mesh):
    parts = Mesh(mesh.devices.reshape(8, 4, 4, 2, 2), ("z", "yh", "x", "yl", "core"))
    return jax.shard_map(
        per_device,
        mesh=parts,
        in_specs=(P(CHAN, SEG), P(CHAN, SEG), P()),
        out_specs=P(SEG, CHAN),
        check_vma=False,
    )
```

```python
import jax
import jax.numpy as jnp
from jax import lax
from jax.experimental import pallas as pl
from jax.experimental.pallas import tpu as pltpu
from jax.sharding import Mesh, PartitionSpec as P

CH = 80
WIN = 1024
WINDOWS = 4
LAGS = 32
SMOOTH = 64
FINE = 4
COARSE = LAGS // FINE
PAD = WIN + 128
PIECES = 32
ROWS = 20
PIECE_ROWS = 24
SENT_ROWS = WINDOWS * ROWS
GROUP = 16
GROUPS = CH // GROUP

CHAN = ("z", "yh", "x")
SEG = ("yl", "core")
SCATTER = ("x", "z")
CROSS = ("core", "yh", "yl")

F32 = jnp.float32
BF16 = jnp.bfloat16
VMEM_LIMIT = 24 * 1024 * 1024


def iota(shape, dim):
    return lax.broadcasted_iota(jnp.int32, shape, dim)


def to_column(row, rows):
    width = row.shape[1]
    spread = jnp.broadcast_to(row, (rows, width))
    diagonal = iota((rows, width), 0) == iota((rows, width), 1)
    return jnp.sum(jnp.where(diagonal, spread, 0.0), axis=1, keepdims=True)


def norm_kernel(strain_ref, alive_ref, pieces_ref, own_ref, full, flags):
    live_row = alive_ref[...].astype(F32)
    live_col = to_column(live_row, CH)
    flags[...] = jnp.zeros((8, 128), F32)
    flags[0:1, 0:CH] = live_row
    position = iota((1, WIN), 1)
    samples_in = (
        jnp.minimum(position, SMOOTH) + jnp.minimum(WIN - 1 - position, SMOOTH) + 1
    ).astype(F32)
    distance = iota((384, 128), 0) - iota((384, 128), 1) - 128
    band = (jnp.abs(distance) <= SMOOTH).astype(F32).astype(BF16)
    edge = jnp.zeros((16, 128), BF16)
    for start in range(0, CH, 16):
        x = strain_ref[start : start + 16, :]
        rest = jnp.abs(x)
        terms = []
        for _ in range(3):
            term = rest.astype(BF16)
            rest = rest - term.astype(F32)
            terms.append(jnp.concatenate([edge, term, edge], axis=1))
        spans = jnp.concatenate(
            [t[:, b * 128 : b * 128 + 384] for t in terms for b in range(8)], axis=0
        )
        sums = jnp.dot(spans, band, preferred_element_type=F32)
        sums = sums[0:128] + sums[128:256] + sums[256:384]
        total = jnp.concatenate([sums[b * 16 : (b + 1) * 16] for b in range(8)], axis=1)
        level = total / samples_in
        normed = x / (level + 1e-5) * live_col[start : start + 16]
        full[start : start + 16, :] = normed
        own_ref[start : start + 16, :] = normed.astype(BF16)
    own_ref[CH : CH + 16, :] = jnp.zeros((16, WIN), BF16)
    own_ref[CH : CH + 16, 0:128] = jnp.concatenate(
        [flags[...], jnp.zeros((8, 128), F32)], axis=0
    ).astype(BF16)
    flag_rows = flags[0 : PIECE_ROWS - ROWS, :]
    for piece in range(PIECES):
        h, q = piece // 8, piece % 8
        data = full[h * ROWS : (h + 1) * ROWS, q * 128 : (q + 1) * 128]
        pieces_ref[piece] = jnp.concatenate([data, flag_rows], axis=0).astype(BF16)


def cross_slot(y, segment):
    return (segment % 2) * 8 + y * 2 + segment // 2


def pick_kernel(plan_ref, got_ref, out_ref):
    for k in range(4):
        block = plan_ref[k]
        holder = (block % 4) * 8 + block // 16
        value = got_ref[holder]
        for y in range(4):
            out_ref[cross_slot(y, k)] = value


def fan_kernel(plan_ref, got_ref, out_ref, flags_ref):
    pair = lax.axis_index("yl") * 2
    block = plan_ref[pair + lax.axis_index("core")]
    y = (block // 4) % 4
    pieces = [got_ref[cross_slot(y, w)].astype(F32) for w in range(WINDOWS)]
    value = jnp.concatenate([p[:ROWS] for p in pieces], axis=0).astype(BF16)
    flag_rows = [p[ROWS : ROWS + 1] for p in pieces] + [jnp.zeros((4, 128), F32)]
    flags_ref[...] = jnp.concatenate(flag_rows, axis=0)
    for copy in range(out_ref.shape[0]):
        out_ref[copy] = value


def correlate_kernel(
    got_ref, own_ref, flags_ref, out_hbm, source, lhs, rhs, total, order, out_ref, sems
):
    row = iota((4 * 128, 4 * 128), 0)
    target = (row % 16) * LAGS + (row // 16 % 8) * FINE + row // 128
    order[...] = (iota((4 * 128, 4 * 128), 1) == target).astype(F32).astype(BF16)
    for w in range(WINDOWS):
        for g in range(GROUPS):
            own = own_ref[w, g * GROUP : (g + 1) * GROUP, :]
            own = jnp.concatenate([own, jnp.zeros((GROUP, PAD - WIN), BF16)], axis=1)
            for b in range(COARSE):
                shift = (LAGS // 2 - FINE * b) % PAD
                moved = own if shift == 0 else pltpu.roll(own, shift, 1)
                first = g * 128 + b * GROUP
                rhs[w, first : first + GROUP, :] = moved
    lane = iota((128, GROUPS * 128), 1)
    channel = (lane // 128) * GROUP + lane % GROUP
    widen = (iota((128, GROUPS * 128), 0) == channel).astype(F32).astype(BF16)
    pairs = jnp.zeros((CH, GROUPS * 128), F32)
    for w in range(WINDOWS):
        own_flags = own_ref[w, CH : CH + 16, 0:128]
        wide = jnp.dot(own_flags, widen, preferred_element_type=F32)[0:1]
        pairs = pairs + to_column(flags_ref[w : w + 1, :], CH) * wide
    pairs = jnp.maximum(pairs, 1.0)
    source[:, :, WIN:] = jnp.zeros((WINDOWS, CH, PAD - WIN), F32)
    for piece in range(PIECES):
        h, q = piece // 8, piece % 8
        value = got_ref[piece].astype(F32)
        for w in range(WINDOWS):
            source[w, h * ROWS : (h + 1) * ROWS, q * 128 : (q + 1) * 128] = value[
                w * ROWS : (w + 1) * ROWS
            ]
    for w in range(WINDOWS):
        block = source[w].astype(BF16)
        for a in range(FINE):
            moved = block if a == 0 else pltpu.roll(block, a, 1)
            lhs[w, a * CH : (a + 1) * CH, :] = moved
    for w in range(WINDOWS):
        partial = lax.dot_general(
            lhs[w], rhs[w], (((1,), (1,)), ((), ())), preferred_element_type=F32
        )
        partial = (partial * (1.0 / WIN)).astype(BF16).astype(F32)
        if w == 0:
            total[...] = partial
        else:
            total[...] += partial
    scaled = [
        (total[a * CH : (a + 1) * CH, :] / pairs).astype(BF16) for a in range(FINE)
    ]
    copies = []
    for g in range(GROUPS):
        mixed = jnp.concatenate([s[:, g * 128 : (g + 1) * 128] for s in scaled], axis=1)
        columns = pl.ds(g * 512, 512)
        out_ref[:, columns] = jnp.dot(
            mixed, order[...], preferred_element_type=F32
        ).astype(BF16)
        copy = pltpu.make_async_copy(
            out_ref.at[:, columns], out_hbm.at[:, columns], sems.at[g]
        )
        copy.start()
        copies.append(copy)
    for copy in copies:
        copy.wait()


def vmem():
    return pl.BlockSpec(memory_space=pltpu.VMEM)


def smem():
    return pl.BlockSpec(memory_space=pltpu.SMEM)


def params():
    return pltpu.CompilerParams(vmem_limit_bytes=VMEM_LIMIT)


def per_device(strain, alive_flags, plan):
    pieces, own = pl.pallas_call(
        norm_kernel,
        out_shape=(
            jax.ShapeDtypeStruct((PIECES, PIECE_ROWS, 128), BF16),
            jax.ShapeDtypeStruct((CH + 16, WIN), BF16),
        ),
        in_specs=[vmem(), vmem()],
        out_specs=(vmem(), vmem()),
        scratch_shapes=[pltpu.VMEM((CH, WIN), F32), pltpu.VMEM((8, 128), F32)],
        compiler_params=params(),
    )(strain, alive_flags.reshape(1, CH))
    scattered = lax.all_to_all(pieces, SCATTER, 0, 0, tiled=True)
    windows = lax.all_gather(own, SEG, axis=0)
    picked = pl.pallas_call(
        pick_kernel,
        out_shape=jax.ShapeDtypeStruct((16, PIECE_ROWS, 128), BF16),
        in_specs=[smem(), vmem()],
        out_specs=vmem(),
        compiler_params=params(),
    )(plan, scattered)
    crossed = lax.all_to_all(picked, CROSS, 0, 0, tiled=True)
    fanned, source_flags = pl.pallas_call(
        fan_kernel,
        out_shape=(
            jax.ShapeDtypeStruct((PIECES, SENT_ROWS, 128), BF16),
            jax.ShapeDtypeStruct((8, 128), F32),
        ),
        in_specs=[smem(), vmem()],
        out_specs=(vmem(), vmem()),
        compiler_params=params(),
    )(plan, crossed)
    gathered = lax.all_to_all(fanned, SCATTER, 0, 0, tiled=True)
    return pl.pallas_call(
        correlate_kernel,
        out_shape=jax.ShapeDtypeStruct((CH, CH * LAGS), BF16),
        in_specs=[vmem()] * 3,
        out_specs=pl.BlockSpec(memory_space=pl.ANY),
        scratch_shapes=[
            pltpu.VMEM((WINDOWS, CH, PAD), F32),
            pltpu.VMEM((WINDOWS, FINE * CH, PAD), BF16),
            pltpu.VMEM((WINDOWS, GROUPS * 128, PAD), BF16),
            pltpu.VMEM((FINE * CH, GROUPS * 128), F32),
            pltpu.VMEM((512, 512), BF16),
            pltpu.VMEM((CH, CH * LAGS), BF16),
            pltpu.SemaphoreType.DMA((GROUPS,)),
        ],
        compiler_params=params(),
        cost_estimate=pl.CostEstimate(flops=3400000000, bytes_accessed=2000000, transcendentals=0),
    )(gathered, windows, source_flags)


def solution(mesh):
    parts = Mesh(mesh.devices.reshape(8, 4, 4, 2, 2), ("z", "yh", "x", "yl", "core"))
    return jax.shard_map(
        per_device,
        mesh=parts,
        in_specs=(P(CHAN, SEG), P(CHAN, SEG), P()),
        out_specs=P(SEG, CHAN),
        check_vma=False,
    )
```

```python
import jax
import jax.numpy as jnp
from jax import lax
from jax.experimental import pallas as pl
from jax.experimental.pallas import tpu as pltpu
from jax.sharding import Mesh, PartitionSpec as P

CH = 80
WIN = 1024
WINDOWS = 4
LAGS = 32
SMOOTH = 64
FINE = 4
COARSE = LAGS // FINE
PAD = WIN + 128
PIECES = 32
ROWS = 20
PIECE_ROWS = 24
SENT_ROWS = WINDOWS * ROWS
GROUP = 16
GROUPS = CH // GROUP

CHAN = ("z2", "z1", "z0", "y1", "y0", "x1", "x0")
SEG = ("yl", "core")
SCATTER = ('x1', 'x0', 'z2', 'z1', 'z0')
GATHER = ('x1', 'x0', 'z1', 'z2', 'z0')
CROSS = ('core', 'y1', 'y0', 'yl')

PLACE = (0, 1, 4, 5, 2, 3, 6, 7, 8, 9, 12, 13, 10, 11, 14, 15, 16, 17, 20, 21, 18, 19, 22, 23, 24, 25, 28, 29, 26, 27, 30, 31)

F32 = jnp.float32
BF16 = jnp.bfloat16
VMEM_LIMIT = 24 * 1024 * 1024


def iota(shape, dim):
    return lax.broadcasted_iota(jnp.int32, shape, dim)


def to_column(row, rows):
    width = row.shape[1]
    spread = jnp.broadcast_to(row, (rows, width))
    diagonal = iota((rows, width), 0) == iota((rows, width), 1)
    return jnp.sum(jnp.where(diagonal, spread, 0.0), axis=1, keepdims=True)


def norm_kernel(strain_ref, alive_ref, pieces_ref, own_ref, full, flags):
    live_row = alive_ref[...].astype(F32)
    live_col = to_column(live_row, CH)
    flags[...] = jnp.zeros((8, 128), F32)
    flags[0:1, 0:CH] = live_row
    position = iota((1, WIN), 1)
    samples_in = (
        jnp.minimum(position, SMOOTH) + jnp.minimum(WIN - 1 - position, SMOOTH) + 1
    ).astype(F32)
    distance = iota((384, 128), 0) - iota((384, 128), 1) - 128
    band = (jnp.abs(distance) <= SMOOTH).astype(F32).astype(BF16)
    edge = jnp.zeros((16, 128), BF16)
    for start in range(0, CH, 16):
        x = strain_ref[start : start + 16, :]
        rest = jnp.abs(x)
        terms = []
        for _ in range(3):
            term = rest.astype(BF16)
            rest = rest - term.astype(F32)
            terms.append(jnp.concatenate([edge, term, edge], axis=1))
        spans = jnp.concatenate(
            [t[:, b * 128 : b * 128 + 384] for t in terms for b in range(8)], axis=0
        )
        sums = jnp.dot(spans, band, preferred_element_type=F32)
        sums = sums[0:128] + sums[128:256] + sums[256:384]
        total = jnp.concatenate([sums[b * 16 : (b + 1) * 16] for b in range(8)], axis=1)
        level = total / samples_in
        normed = x / (level + 1e-5) * live_col[start : start + 16]
        full[start : start + 16, :] = normed
        own_ref[start : start + 16, :] = normed.astype(BF16)
    own_ref[CH : CH + 16, :] = jnp.zeros((16, WIN), BF16)
    own_ref[CH : CH + 16, 0:128] = jnp.concatenate(
        [flags[...], jnp.zeros((8, 128), F32)], axis=0
    ).astype(BF16)
    flag_rows = flags[0 : PIECE_ROWS - ROWS, :]
    for piece in range(PIECES):
        q, h = piece // 4, piece % 4
        data = full[h * ROWS : (h + 1) * ROWS, q * 128 : (q + 1) * 128]
        pieces_ref[piece] = jnp.concatenate([data, flag_rows], axis=0).astype(BF16)


def pick_kernel(plan_ref, got_ref, out_ref):
    for k in range(4):
        block = plan_ref[k]
        holder = (block // 2 % 2) * 16 + (block % 2) * 8 + (block // 64 % 2) * 4 + (block // 32 % 2) * 2 + (block // 16 % 2)
        value = got_ref[holder]
        for y in range(4):
            out_ref[4 * (y // 2) + 2 * (y % 2) + 1 * (k // 2) + 8 * (k % 2)] = value


def fan_kernel(plan_ref, got_ref, out_ref, flags_ref):
    pair = lax.axis_index("yl") * 2
    block = plan_ref[pair + lax.axis_index("core")]
    y = (block // 4) % 4
    pieces = [got_ref[4 * (y // 2) + 2 * (y % 2) + 1 * (w // 2) + 8 * (w % 2)].astype(F32) for w in range(WINDOWS)]
    value = jnp.concatenate([p[:ROWS] for p in pieces], axis=0).astype(BF16)
    flag_rows = [p[ROWS : ROWS + 1] for p in pieces] + [jnp.zeros((4, 128), F32)]
    flags_ref[...] = jnp.concatenate(flag_rows, axis=0)
    for copy in range(out_ref.shape[0]):
        out_ref[copy] = value


def correlate_kernel(
    got_ref, own_ref, flags_ref, out_hbm, source, lhs, rhs, total, order, out_ref, sems
):
    row = iota((4 * 128, 4 * 128), 0)
    target = (row % 16) * LAGS + (row // 16 % 8) * FINE + row // 128
    order[...] = (iota((4 * 128, 4 * 128), 1) == target).astype(F32).astype(BF16)
    for w in range(WINDOWS):
        for g in range(GROUPS):
            own = own_ref[w, g * GROUP : (g + 1) * GROUP, :]
            own = jnp.concatenate([own, jnp.zeros((GROUP, PAD - WIN), BF16)], axis=1)
            for b in range(COARSE):
                shift = (LAGS // 2 - FINE * b) % PAD
                moved = own if shift == 0 else pltpu.roll(own, shift, 1)
                first = g * 128 + b * GROUP
                rhs[w, first : first + GROUP, :] = moved
    lane = iota((128, GROUPS * 128), 1)
    channel = (lane // 128) * GROUP + lane % GROUP
    widen = (iota((128, GROUPS * 128), 0) == channel).astype(F32).astype(BF16)
    pairs = jnp.zeros((CH, GROUPS * 128), F32)
    for w in range(WINDOWS):
        own_flags = own_ref[w, CH : CH + 16, 0:128]
        wide = jnp.dot(own_flags, widen, preferred_element_type=F32)[0:1]
        pairs = pairs + to_column(flags_ref[w : w + 1, :], CH) * wide
    pairs = jnp.maximum(pairs, 1.0)
    source[:, :, WIN:] = jnp.zeros((WINDOWS, CH, PAD - WIN), F32)
    for piece in range(PIECES):
        q, h = PLACE[piece] // 4, PLACE[piece] % 4
        value = got_ref[piece].astype(F32)
        for w in range(WINDOWS):
            source[w, h * ROWS : (h + 1) * ROWS, q * 128 : (q + 1) * 128] = value[
                w * ROWS : (w + 1) * ROWS
            ]
    for w in range(WINDOWS):
        block = source[w].astype(BF16)
        for a in range(FINE):
            moved = block if a == 0 else pltpu.roll(block, a, 1)
            lhs[w, a * CH : (a + 1) * CH, :] = moved
    for w in range(WINDOWS):
        partial = lax.dot_general(
            lhs[w], rhs[w], (((1,), (1,)), ((), ())), preferred_element_type=F32
        )
        partial = (partial * (1.0 / WIN)).astype(BF16).astype(F32)
        if w == 0:
            total[...] = partial
        else:
            total[...] += partial
    scaled = [
        (total[a * CH : (a + 1) * CH, :] / pairs).astype(BF16) for a in range(FINE)
    ]
    copies = []
    for g in range(GROUPS):
        mixed = jnp.concatenate([s[:, g * 128 : (g + 1) * 128] for s in scaled], axis=1)
        columns = pl.ds(g * 512, 512)
        out_ref[:, columns] = jnp.dot(
            mixed, order[...], preferred_element_type=F32
        ).astype(BF16)
        copy = pltpu.make_async_copy(
            out_ref.at[:, columns], out_hbm.at[:, columns], sems.at[g]
        )
        copy.start()
        copies.append(copy)
    for copy in copies:
        copy.wait()


def vmem():
    return pl.BlockSpec(memory_space=pltpu.VMEM)


def smem():
    return pl.BlockSpec(memory_space=pltpu.SMEM)


def params():
    return pltpu.CompilerParams(vmem_limit_bytes=VMEM_LIMIT)


def per_device(strain, alive_flags, plan):
    pieces, own = pl.pallas_call(
        norm_kernel,
        out_shape=(
            jax.ShapeDtypeStruct((PIECES, PIECE_ROWS, 128), BF16),
            jax.ShapeDtypeStruct((CH + 16, WIN), BF16),
        ),
        in_specs=[vmem(), vmem()],
        out_specs=(vmem(), vmem()),
        scratch_shapes=[pltpu.VMEM((CH, WIN), F32), pltpu.VMEM((8, 128), F32)],
        compiler_params=params(),
    )(strain, alive_flags.reshape(1, CH))
    scattered = lax.all_to_all(pieces, SCATTER, 0, 0, tiled=True)
    windows = lax.all_gather(own, SEG, axis=0)
    picked = pl.pallas_call(
        pick_kernel,
        out_shape=jax.ShapeDtypeStruct((16, PIECE_ROWS, 128), BF16),
        in_specs=[smem(), vmem()],
        out_specs=vmem(),
        compiler_params=params(),
    )(plan, scattered)
    crossed = lax.all_to_all(picked, CROSS, 0, 0, tiled=True)
    fanned, source_flags = pl.pallas_call(
        fan_kernel,
        out_shape=(
            jax.ShapeDtypeStruct((PIECES, SENT_ROWS, 128), BF16),
            jax.ShapeDtypeStruct((8, 128), F32),
        ),
        in_specs=[smem(), vmem()],
        out_specs=(vmem(), vmem()),
        compiler_params=params(),
    )(plan, crossed)
    gathered = lax.all_to_all(fanned, GATHER, 0, 0, tiled=True)
    return pl.pallas_call(
        correlate_kernel,
        out_shape=jax.ShapeDtypeStruct((CH, CH * LAGS), BF16),
        in_specs=[vmem()] * 3,
        out_specs=pl.BlockSpec(memory_space=pl.ANY),
        scratch_shapes=[
            pltpu.VMEM((WINDOWS, CH, PAD), F32),
            pltpu.VMEM((WINDOWS, FINE * CH, PAD), BF16),
            pltpu.VMEM((WINDOWS, GROUPS * 128, PAD), BF16),
            pltpu.VMEM((FINE * CH, GROUPS * 128), F32),
            pltpu.VMEM((512, 512), BF16),
            pltpu.VMEM((CH, CH * LAGS), BF16),
            pltpu.SemaphoreType.DMA((GROUPS,)),
        ],
        compiler_params=params(),
        cost_estimate=pl.CostEstimate(flops=3400000000, bytes_accessed=2000000, transcendentals=0),
    )(gathered, windows, source_flags)


def solution(mesh):
    parts = Mesh(mesh.devices.reshape((2,) * 9), CHAN + SEG)
    return jax.shard_map(
        per_device,
        mesh=parts,
        in_specs=(P(CHAN, SEG), P(CHAN, SEG), P()),
        out_specs=P(SEG, CHAN),
        check_vma=False,
    )
```

```python
import jax
import jax.numpy as jnp
from jax import lax
from jax.experimental import pallas as pl
from jax.experimental.pallas import tpu as pltpu
from jax.sharding import Mesh, PartitionSpec as P

CH = 80
WIN = 1024
WINDOWS = 4
LAGS = 32
SMOOTH = 64
FINE = 4
COARSE = LAGS // FINE
PAD = WIN + 128
PIECES = 32
ROWS = 20
PIECE_ROWS = 24
SENT_ROWS = WINDOWS * ROWS
GROUP = 16
GROUPS = CH // GROUP

CHAN = ("z2", "z1", "z0", "y1", "y0", "x1", "x0")
SEG = ("yl", "core")
SCATTER = ('x1', 'x0', 'z1', 'z2', 'z0')
GATHER = ('x1', 'x0', 'z1', 'z2', 'z0')
CROSS = ('core', 'y1', 'y0', 'yl')

F32 = jnp.float32
BF16 = jnp.bfloat16
VMEM_LIMIT = 24 * 1024 * 1024


def iota(shape, dim):
    return lax.broadcasted_iota(jnp.int32, shape, dim)


def to_column(row, rows):
    width = row.shape[1]
    spread = jnp.broadcast_to(row, (rows, width))
    diagonal = iota((rows, width), 0) == iota((rows, width), 1)
    return jnp.sum(jnp.where(diagonal, spread, 0.0), axis=1, keepdims=True)


def norm_kernel(strain_ref, alive_ref, pieces_ref, own_ref, full, flags):
    live_row = alive_ref[...].astype(F32)
    live_col = to_column(live_row, CH)
    flags[...] = jnp.zeros((8, 128), F32)
    flags[0:1, 0:CH] = live_row
    position = iota((1, WIN), 1)
    samples_in = (
        jnp.minimum(position, SMOOTH) + jnp.minimum(WIN - 1 - position, SMOOTH) + 1
    ).astype(F32)
    distance = iota((384, 128), 0) - iota((384, 128), 1) - 128
    band = (jnp.abs(distance) <= SMOOTH).astype(F32).astype(BF16)
    edge = jnp.zeros((16, 128), BF16)
    for start in range(0, CH, 16):
        x = strain_ref[start : start + 16, :]
        rest = jnp.abs(x)
        terms = []
        for _ in range(3):
            term = rest.astype(BF16)
            rest = rest - term.astype(F32)
            terms.append(jnp.concatenate([edge, term, edge], axis=1))
        spans = jnp.concatenate(
            [t[:, b * 128 : b * 128 + 384] for t in terms for b in range(8)], axis=0
        )
        sums = jnp.dot(spans, band, preferred_element_type=F32)
        sums = sums[0:128] + sums[128:256] + sums[256:384]
        total = jnp.concatenate([sums[b * 16 : (b + 1) * 16] for b in range(8)], axis=1)
        level = total / samples_in
        normed = x / (level + 1e-5) * live_col[start : start + 16]
        full[start : start + 16, :] = normed
        own_ref[start : start + 16, :] = normed.astype(BF16)
    own_ref[CH : CH + 16, :] = jnp.zeros((16, WIN), BF16)
    own_ref[CH : CH + 16, 0:128] = jnp.concatenate(
        [flags[...], jnp.zeros((8, 128), F32)], axis=0
    ).astype(BF16)
    flag_rows = flags[0 : PIECE_ROWS - ROWS, :]
    for piece in range(PIECES):
        q, h = piece // 4, piece % 4
        data = full[h * ROWS : (h + 1) * ROWS, q * 128 : (q + 1) * 128]
        pieces_ref[piece] = jnp.concatenate([data, flag_rows], axis=0).astype(BF16)


def pick_kernel(plan_ref, got_ref, out_ref):
    for k in range(4):
        block = plan_ref[k]
        holder = (block // 2 % 2) * 16 + (block % 2) * 8 + (block // 32 % 2) * 4 + (block // 64 % 2) * 2 + (block // 16 % 2)
        value = got_ref[holder]
        for y in range(4):
            out_ref[4 * (y // 2) + 2 * (y % 2) + 1 * (k // 2) + 8 * (k % 2)] = value


def fan_kernel(plan_ref, got_ref, out_ref, flags_ref):
    pair = lax.axis_index("yl") * 2
    block = plan_ref[pair + lax.axis_index("core")]
    y = (block // 4) % 4
    pieces = [got_ref[4 * (y // 2) + 2 * (y % 2) + 1 * (w // 2) + 8 * (w % 2)].astype(F32) for w in range(WINDOWS)]
    value = jnp.concatenate([p[:ROWS] for p in pieces], axis=0).astype(BF16)
    flag_rows = [p[ROWS : ROWS + 1] for p in pieces] + [jnp.zeros((4, 128), F32)]
    flags_ref[...] = jnp.concatenate(flag_rows, axis=0)
    for copy in range(out_ref.shape[0]):
        out_ref[copy] = value


def correlate_kernel(
    got_ref, own_ref, flags_ref, out_hbm, source, lhs, rhs, total, order, out_ref, sems
):
    row = iota((4 * 128, 4 * 128), 0)
    target = (row % 16) * LAGS + (row // 16 % 8) * FINE + row // 128
    order[...] = (iota((4 * 128, 4 * 128), 1) == target).astype(F32).astype(BF16)
    for w in range(WINDOWS):
        for g in range(GROUPS):
            own = own_ref[w, g * GROUP : (g + 1) * GROUP, :]
            own = jnp.concatenate([own, jnp.zeros((GROUP, PAD - WIN), BF16)], axis=1)
            for b in range(COARSE):
                shift = (LAGS // 2 - FINE * b) % PAD
                moved = own if shift == 0 else pltpu.roll(own, shift, 1)
                first = g * 128 + b * GROUP
                rhs[w, first : first + GROUP, :] = moved
    lane = iota((128, GROUPS * 128), 1)
    channel = (lane // 128) * GROUP + lane % GROUP
    widen = (iota((128, GROUPS * 128), 0) == channel).astype(F32).astype(BF16)
    pairs = jnp.zeros((CH, GROUPS * 128), F32)
    for w in range(WINDOWS):
        own_flags = own_ref[w, CH : CH + 16, 0:128]
        wide = jnp.dot(own_flags, widen, preferred_element_type=F32)[0:1]
        pairs = pairs + to_column(flags_ref[w : w + 1, :], CH) * wide
    pairs = jnp.maximum(pairs, 1.0)
    source[:, :, WIN:] = jnp.zeros((WINDOWS, CH, PAD - WIN), F32)
    for piece in range(PIECES):
        q, h = piece // 4, piece % 4
        value = got_ref[piece].astype(F32)
        for w in range(WINDOWS):
            source[w, h * ROWS : (h + 1) * ROWS, q * 128 : (q + 1) * 128] = value[
                w * ROWS : (w + 1) * ROWS
            ]
    for w in range(WINDOWS):
        block = source[w].astype(BF16)
        for a in range(FINE):
            moved = block if a == 0 else pltpu.roll(block, a, 1)
            lhs[w, a * CH : (a + 1) * CH, :] = moved
    for w in range(WINDOWS):
        partial = lax.dot_general(
            lhs[w], rhs[w], (((1,), (1,)), ((), ())), preferred_element_type=F32
        )
        partial = (partial * (1.0 / WIN)).astype(BF16).astype(F32)
        if w == 0:
            total[...] = partial
        else:
            total[...] += partial
    scaled = [
        (total[a * CH : (a + 1) * CH, :] / pairs).astype(BF16) for a in range(FINE)
    ]
    copies = []
    for g in range(GROUPS):
        mixed = jnp.concatenate([s[:, g * 128 : (g + 1) * 128] for s in scaled], axis=1)
        columns = pl.ds(g * 512, 512)
        out_ref[:, columns] = jnp.dot(
            mixed, order[...], preferred_element_type=F32
        ).astype(BF16)
        copy = pltpu.make_async_copy(
            out_ref.at[:, columns], out_hbm.at[:, columns], sems.at[g]
        )
        copy.start()
        copies.append(copy)
    for copy in copies:
        copy.wait()


def vmem():
    return pl.BlockSpec(memory_space=pltpu.VMEM)


def smem():
    return pl.BlockSpec(memory_space=pltpu.SMEM)


def params():
    return pltpu.CompilerParams(vmem_limit_bytes=VMEM_LIMIT)


def per_device(strain, alive_flags, plan):
    pieces, own = pl.pallas_call(
        norm_kernel,
        out_shape=(
            jax.ShapeDtypeStruct((PIECES, PIECE_ROWS, 128), BF16),
            jax.ShapeDtypeStruct((CH + 16, WIN), BF16),
        ),
        in_specs=[vmem(), vmem()],
        out_specs=(vmem(), vmem()),
        scratch_shapes=[pltpu.VMEM((CH, WIN), F32), pltpu.VMEM((8, 128), F32)],
        compiler_params=params(),
    )(strain, alive_flags.reshape(1, CH))
    scattered = lax.all_to_all(pieces, SCATTER, 0, 0, tiled=True)
    windows = lax.all_gather(own, SEG, axis=0)
    picked = pl.pallas_call(
        pick_kernel,
        out_shape=jax.ShapeDtypeStruct((16, PIECE_ROWS, 128), BF16),
        in_specs=[smem(), vmem()],
        out_specs=vmem(),
        compiler_params=params(),
    )(plan, scattered)
    crossed = lax.all_to_all(picked, CROSS, 0, 0, tiled=True)
    fanned, source_flags = pl.pallas_call(
        fan_kernel,
        out_shape=(
            jax.ShapeDtypeStruct((PIECES, SENT_ROWS, 128), BF16),
            jax.ShapeDtypeStruct((8, 128), F32),
        ),
        in_specs=[smem(), vmem()],
        out_specs=(vmem(), vmem()),
        compiler_params=params(),
    )(plan, crossed)
    gathered = lax.all_to_all(fanned, GATHER, 0, 0, tiled=True)
    return pl.pallas_call(
        correlate_kernel,
        out_shape=jax.ShapeDtypeStruct((CH, CH * LAGS), BF16),
        in_specs=[vmem()] * 3,
        out_specs=pl.BlockSpec(memory_space=pl.ANY),
        scratch_shapes=[
            pltpu.VMEM((WINDOWS, CH, PAD), F32),
            pltpu.VMEM((WINDOWS, FINE * CH, PAD), BF16),
            pltpu.VMEM((WINDOWS, GROUPS * 128, PAD), BF16),
            pltpu.VMEM((FINE * CH, GROUPS * 128), F32),
            pltpu.VMEM((512, 512), BF16),
            pltpu.VMEM((CH, CH * LAGS), BF16),
            pltpu.SemaphoreType.DMA((GROUPS,)),
        ],
        compiler_params=params(),
        cost_estimate=pl.CostEstimate(flops=3400000000, bytes_accessed=2000000, transcendentals=0),
    )(gathered, windows, source_flags)


def solution(mesh):
    parts = Mesh(mesh.devices.reshape((2,) * 9), CHAN + SEG)
    return jax.shard_map(
        per_device,
        mesh=parts,
        in_specs=(P(CHAN, SEG), P(CHAN, SEG), P()),
        out_specs=P(SEG, CHAN),
        check_vma=False,
    )
```
